256 devices in a mesh: dp: 64 (over z, y, x_lo), fsdp: 4 (over x_hi, core).
Axes of the slice: x: 4 (x_hi: 2, x_lo: 2; x = x_hi * 2 + x_lo), y: 4, z: 8, core: 2. Of those that a mesh axis runs over, the one named last changes fastest.
Arguments:
- context: bfloat16 [32768, 3328], P(('dp', 'fsdp')), may hold values from -140 to 140
- upstream: bfloat16 [32768, 3328], P(('dp', 'fsdp')), may hold values from -1000 to 1000
- weight: bfloat16 [3328, 3328], P('fsdp'), may hold values from -0.109375 to 0.109375
Outputs:
- d_context: bfloat16 [32768, 3328], P(('dp', 'fsdp'))
- combined: bfloat16 [3328, 3328], P('fsdp', 'dp')
The draws below stay inside these ranges and needn't reach their ends.
All inputs are finite; a program needn't handle non-finite values.
Results may differ from the reference program's by a relative error of at most 0.0062.
Values may be sent and summed in bfloat16 or wider, within the bound.
No kernel may reach another device: no remote copies, remote signals or barrier semaphores. Data moves between devices by JAX's collectives and lax.ppermute only.
A program may use at most 128 MiB of HBM per device.

```python
import jax
import jax.numpy as jnp
from jax import lax

HD = 3328
DW = 3328
TOK_REP = 512
TOKENS = 32768
FEAT_DEV = 832
LEVELS = 6


def assemble(common, own, row_scale, width, col_key, weight_common, weight_own, rough_lo, rough_hi):
    ramp = 10.0 ** (jnp.arange(width, dtype=jnp.float32) / width)
    rough = jnp.exp(jax.random.uniform(col_key, (width,), jnp.float32, jnp.log(rough_lo), jnp.log(rough_hi)))
    tiled = jnp.tile(common, (TOKENS // TOK_REP, 1))
    full = weight_common * tiled + weight_own * own
    return (full * (ramp * rough)[None, :] * row_scale).astype(jnp.bfloat16)


def block_mix(perm_key):
    count = HD // FEAT_DEV
    steps_up = jnp.arange(count, dtype=jnp.float32) / float(max(count - 1, 1))
    levels_mix = 0.3 + 0.65 * steps_up
    order = jax.random.permutation(perm_key, count)
    chosen = levels_mix[order]
    per_feature = jnp.repeat(chosen, FEAT_DEV)
    return (per_feature, jnp.sqrt(1.0 - per_feature * per_feature))


def column_mix(perm_key, jitter_key):
    count = TOKENS // TOK_REP
    block_width = DW // count
    steps_up = jnp.arange(count, dtype=jnp.float32) / float(max(count - 1, 1))
    levels_mix = 0.3 + 0.65 * steps_up
    order = jax.random.permutation(perm_key, count)
    per_column = jnp.repeat(levels_mix[order], block_width)
    jitter = jax.random.uniform(jitter_key, (DW,), jnp.float32, 0.3, 1.0)
    mixed = per_column * jitter
    return (mixed, jnp.sqrt(1.0 - mixed * mixed))


def replica_scale(scale_key):
    count = TOKENS // TOK_REP
    per_replica = jnp.exp(jax.random.uniform(scale_key, (count, 1), jnp.float32, jnp.log(0.5), jnp.log(2.0)))
    return jnp.repeat(per_replica, TOK_REP, axis=0)


def draw_context(key, part):
    key = jax.random.fold_in(key, 11)
    first = jax.random.fold_in(key, 0)
    second = jax.random.fold_in(key, 1)
    third = jax.random.fold_in(key, 2)
    fifth = jax.random.fold_in(key, 4)
    mix_common, mix_own = block_mix(fifth)
    common = jax.random.truncated_normal(first, -4.0, 4.0, (TOK_REP, HD), jnp.float32)
    own = jax.random.truncated_normal(second, -4.0, 4.0, (TOKENS, HD), jnp.float32)
    return assemble(common, own, 1.0, HD, third, mix_common, mix_own, 0.7, 1.4)


def draw_upstream(key, part):
    key = jax.random.fold_in(key, 23)
    first = jax.random.fold_in(key, 0)
    second = jax.random.fold_in(key, 1)
    third = jax.random.fold_in(key, 2)
    fifth = jax.random.fold_in(key, 4)
    sixth = jax.random.fold_in(key, 5)
    seventh = jax.random.fold_in(key, 6)
    mix_common, mix_own = column_mix(fifth, sixth)
    replicas = replica_scale(seventh)
    common = jax.random.truncated_normal(first, -4.0, 4.0, (TOK_REP, DW), jnp.float32)
    own = jax.random.truncated_normal(second, -4.0, 4.0, (TOKENS, DW), jnp.float32)
    return assemble(common, own, replicas, DW, third, mix_common, mix_own, 0.2, 5.0)


def levels(stream_key, dims, cuts, smallest, largest):
    factor_of, own = 1.0, jax.random.fold_in(stream_key, 6)
    for axis_at, shards_of in cuts:
        heights = jnp.exp(jax.random.uniform(jax.random.fold_in(own, axis_at), (shards_of,), jnp.float32, smallest / len(cuts), largest / len(cuts)))
        factor_of = factor_of * jnp.repeat(heights, dims[axis_at] // shards_of).reshape([-1 if axis == axis_at else 1 for axis in range(len(dims))])
    return factor_of


def gaussian(key, extent, scale, reach, cuts=(), kind=jnp.bfloat16):
    entries = scale * jax.random.normal(key, extent, jnp.float32)
    if cuts:
        entries = entries * levels(key, extent, cuts, -0.22, 0.18)
    return jnp.clip(entries, -reach, reach).astype(kind)


def setup_inputs(seed: int = 0) -> dict:
    key_of = jax.random.split(jax.random.key(seed), 4)
    context = draw_context(jax.random.fold_in(key_of[3], 71), 0)
    upstream = draw_upstream(jax.random.fold_in(key_of[3], 71), 0)
    weight = gaussian(key_of[2], (HD, DW), DW ** -0.5, 0.109375, ((0, 4),))
    return dict(context=context, upstream=upstream, weight=weight)


def replica_grad(pair):
    ctx, up = pair
    prod = lax.dot_general(ctx, up, (((0,), (0,)), ((), ())), preferred_element_type=jnp.float32)
    return (prod / TOK_REP).astype(jnp.bfloat16)

def pair_mix(pair):
    lower = pair[0].astype(jnp.float32)
    upper = pair[1].astype(jnp.float32)
    norm_a = jnp.sum(lower * lower)
    norm_b = jnp.sum(upper * upper)
    cross = jnp.sum(lower * upper)
    coef_a = 1.0 - cross / (2.0 * norm_a)
    coef_b = 1.0 - cross / (2.0 * norm_b)
    return (coef_a * lower + coef_b * upper).astype(jnp.bfloat16)

def reference(context, upstream, weight):
    d_context = jnp.dot(upstream, weight.T, preferred_element_type=jnp.float32).astype(jnp.bfloat16)
    ctx = context.reshape(TOKENS // TOK_REP, TOK_REP, HD)
    ups = upstream.reshape(TOKENS // TOK_REP, TOK_REP, DW)
    vectors = lax.map(replica_grad, (ctx, ups))
    for level in range(LEVELS):
        vectors = lax.map(pair_mix, vectors.reshape(-1, 2, HD, DW))
    return (d_context, vectors[0])
```

```python
import jax
import jax.numpy as jnp
import numpy as np
from jax import lax
from jax.sharding import Mesh
from jax.sharding import PartitionSpec as P

AXES = ("z", "y", "xl", "xh", "c")
SIZES = (8, 4, 2, 2, 2)
BF16 = jnp.bfloat16
F32 = jnp.float32


def routes(where_to):
    pairs = []
    for source, (z, y, xl, xh, c) in enumerate(np.ndindex(*SIZES)):
        z2, y2, x2, c2 = where_to(z, y, 2 * xh + xl, c)
        place = (z2 % 8, y2 % 4, x2 & 1, x2 >> 1, c2)
        pairs.append((source, int(np.ravel_multi_index(place, SIZES))))
    return pairs


SIB = routes(lambda z, y, x, c: (z, y, x ^ 1, c))
MATE = routes(lambda z, y, x, c: (z, y, 3 - x, c))
OPP = routes(lambda z, y, x, c: (z, y, x ^ 2, c))
CHIP = routes(lambda z, y, x, c: (z, y, x, 1 - c))
Y_SHIFT = [routes(lambda z, y, x, c, d=d: (z, y + d, x, c)) for d in range(4)]
Z_SHIFT = [routes(lambda z, y, x, c, d=d: (z + d, y, x, c)) for d in range(8)]


def final_place(z, y, x, c):
    block = ((x & 1) ^ (x >> 1)) * 32 + y * 8 + z
    return (block >> 3, (block >> 1) & 3, (x & 2) | (block & 1), c)


FINAL = routes(final_place)


def send(value, pairs):
    return lax.ppermute(value, AXES, pairs)


def sum_x(s):
    s = s + send(s, CHIP)
    return s + send(s, SIB) + send(s, MATE) + send(s, OPP)


def sum_y(s):
    return s + send(s, Y_SHIFT[1]) + send(s, Y_SHIFT[2]) + send(s, Y_SHIFT[3])


def sum_z(s):
    return s + sum(send(s, Z_SHIFT[d]) for d in range(1, 8))


def tree_coefs(gram):
    count = gram.shape[0]
    rows = [[gram[i, j] for j in range(count)] for i in range(count)]
    coefs = [jnp.float32(1.0)] * count
    while len(rows) > 1:
        half = len(rows) // 2
        pair = []
        for k in range(half):
            cross = rows[2 * k][2 * k + 1]
            pair.append((1.0 - cross / (2.0 * rows[2 * k][2 * k]), 1.0 - cross / (2.0 * rows[2 * k + 1][2 * k + 1])))
        span = count // len(rows)
        coefs = [coefs[i] * pair[i // (2 * span)][(i // span) % 2] for i in range(count)]
        rows = [
            [
                sum(pair[k][p] * pair[m][q] * rows[2 * k + p][2 * m + q] for p in range(2) for q in range(2))
                for m in range(half)
            ]
            for k in range(half)
        ]
    return jnp.stack(coefs)


def gram_of(vectors):
    wide = vectors.astype(F32)
    count = vectors.shape[0]
    sums = [[None] * count for _ in range(count)]
    for i in range(count):
        for j in range(i, count):
            sums[i][j] = sums[j][i] = jnp.sum(wide[i] * wide[j])
    return jnp.stack([jnp.stack(row) for row in sums])


def combine(coefs, vectors):
    return sum(coefs[i] * vectors[i].astype(F32) for i in range(vectors.shape[0])).astype(BF16)


def on_device(context, upstream, weight):
    tokens = context.shape[0]
    half = context.shape[1] // 2
    quarter = half // 2
    z, y = lax.axis_index("z"), lax.axis_index("y")
    xl, xh, core = lax.axis_index("xl"), lax.axis_index("xh"), lax.axis_index("c")
    d_half = xl ^ xh
    pick = lambda flag, a, b: jnp.where(flag == 1, b, a)

    u0, u1 = upstream[:, :half], upstream[:, half:]
    c0, c1 = context[:, :half], context[:, half:]
    u_own, u_rest = pick(d_half, u0, u1), pick(d_half, u1, u0)
    c_own, c_rest = pick(xh, c0, c1), pick(xh, c1, c0)
    u_sib = send(u_rest, SIB)
    c_mate = send(c_rest, MATE)
    c_sib = send(c_own, SIB)
    u_mate = send(u_own, MATE)
    c_opp = send(c_mate, SIB)
    u_opp = send(u_sib, MATE)
    u_mate_rest = send(u_rest, MATE)

    def both_cores(value):
        return jnp.concatenate([value, send(value, CHIP)], 0)

    def quarters(value):
        keep = pick(core, value[:, :quarter], value[:, quarter:])
        give = pick(core, value[:, quarter:], value[:, :quarter])
        return jnp.concatenate([keep, send(give, CHIP)], 0)

    def grad(us, cs):
        u = jnp.concatenate([both_cores(u) for u in us], 0)
        c = jnp.concatenate([quarters(c) for c in cs], 0)
        total = lax.dot_general(u, c, (((0,), (0,)), ((), ())), preferred_element_type=F32)
        return (total / (4 * tokens)).astype(BF16)

    other = grad([u_sib, u_mate], [c_sib, c_mate])
    own = grad([u_own, u_opp], [c_own, c_opp])
    gram = gram_of(jnp.stack([own, other]))
    gram = pick(xl, gram, gram[::-1, ::-1])
    gram = sum_x(gram)
    coefs = tree_coefs(pick(xl, gram, gram[::-1, ::-1]))
    vector = (coefs[0] * own.astype(F32) + coefs[1] * other.astype(F32)).astype(BF16)

    u_a = jnp.concatenate([both_cores(u_own), both_cores(u_mate)], 0)
    u_b = jnp.concatenate([both_cores(u_rest), both_cores(u_mate_rest)], 0)
    wide = jnp.concatenate([pick(d_half, u_a, u_b), pick(d_half, u_b, u_a)], 1)
    back = lax.dot_general(wide, weight, (((1,), (1,)), ((), ())), preferred_element_type=F32).astype(BF16)

    def token_rows(value):
        mine, theirs = value[:tokens], send(value[tokens:], CHIP)
        return jnp.concatenate([pick(core, mine, theirs), pick(core, theirs, mine)], 1)

    near = token_rows(back[: 2 * tokens])
    far = send(token_rows(back[2 * tokens :]), MATE)
    d_context = jnp.concatenate([pick(xh, near, far), pick(xh, far, near)], 1)

    rows_y = vector.shape[0] // 4
    piece = lambda k: lax.dynamic_slice_in_dim(vector, (k % 4) * rows_y, rows_y, 0)
    parts = [piece(y)] + [send(piece(y + d), Y_SHIFT[d]) for d in range(1, 4)]
    stack = jnp.stack(parts)
    order = lambda g: g[(y - jnp.arange(4)) % 4]
    stack = order(stack)
    gram = sum_x(sum_y(gram_of(stack)))
    vector = combine(tree_coefs(gram), stack)

    rows_z = vector.shape[0] // 8
    piece_z = lambda k: lax.dynamic_slice_in_dim(vector, (k % 8) * rows_z, rows_z, 0)
    parts = [piece_z(z)] + [send(piece_z(z + d), Z_SHIFT[d]) for d in range(1, 8)]
    stack = jnp.stack(parts)[(z - jnp.arange(8)) % 8]
    gram = sum_z(sum_x(sum_y(gram_of(stack))))
    vector = combine(tree_coefs(gram), stack)
    return d_context, send(vector, FINAL).T


def solution(mesh):
    fine = Mesh(mesh.devices.reshape(SIZES), AXES)
    return jax.shard_map(
        on_device,
        mesh=fine,
        in_specs=(P(AXES, None), P(AXES, None), P(("xh", "c"), None)),
        out_specs=(P(AXES, None), P(("xh", "c"), ("z", "y", "xl"))),
        check_vma=False,
    )
```

```python
import jax
import jax.numpy as jnp
import numpy as np
from jax import lax
from jax.experimental import pallas as pl
from jax.experimental.pallas import tpu as pltpu
from jax.sharding import Mesh
from jax.sharding import PartitionSpec as P

AXES = ("z", "y", "xl", "xh", "c")
SIZES = (8, 4, 2, 2, 2)
BF16 = jnp.bfloat16
F32 = jnp.float32


def routes(where_to):
    pairs = []
    for source, (z, y, xl, xh, c) in enumerate(np.ndindex(*SIZES)):
        z2, y2, x2, c2 = where_to(z, y, 2 * xh + xl, c)
        place = (z2 % 8, y2 % 4, x2 & 1, x2 >> 1, c2)
        pairs.append((source, int(np.ravel_multi_index(place, SIZES))))
    return pairs


SIB = routes(lambda z, y, x, c: (z, y, x ^ 1, c))
MATE = routes(lambda z, y, x, c: (z, y, 3 - x, c))
OPP = routes(lambda z, y, x, c: (z, y, x ^ 2, c))
CHIP = routes(lambda z, y, x, c: (z, y, x, 1 - c))
Y_SHIFT = [routes(lambda z, y, x, c, d=d: (z, y + d, x, c)) for d in range(4)]
Z_SHIFT = [routes(lambda z, y, x, c, d=d: (z + d, y, x, c)) for d in range(8)]
Z_SPLIT = [routes(lambda z, y, x, c, d=d: (z - d if c else z + d, y, x, c)) for d in (1, 2, 3)]
Z_SPLIT.append([(a, b) for a, b in Z_SHIFT[4] if a % 2])


def final_place(z, y, x, c):
    block = ((x & 1) ^ (x >> 1)) * 32 + y * 8 + z
    return (block >> 3, (block >> 1) & 3, (x & 2) | (block & 1), c)


FINAL = routes(final_place)


def send(value, pairs):
    return lax.ppermute(value, AXES, pairs)


def sum_x(s):
    s = s + send(s, CHIP)
    return s + send(s, SIB) + send(s, MATE) + send(s, OPP)


def sum_y(s):
    return s + send(s, Y_SHIFT[1]) + send(s, Y_SHIFT[2]) + send(s, Y_SHIFT[3])


def sum_z(s):
    own = jnp.where(lax.axis_index("c") == 0, s, 0.0)
    s = own + sum(send(s, pairs) for pairs in Z_SPLIT)
    return s + send(s, CHIP)


def tree_coefs(rows):
    count = len(rows)
    coefs = [1.0] * count
    while len(rows) > 1:
        half = len(rows) // 2
        span = count // len(rows)
        pair = []
        for k in range(half):
            cross = rows[2 * k][2 * k + 1]
            pair.append([1.0 - cross / (2.0 * rows[2 * k + p][2 * k + p]) for p in range(2)])
        coefs = [coefs[i] * pair[i // (2 * span)][(i // span) % 2] for i in range(count)]
        rows = [
            [
                sum(pair[k][p] * pair[m][q] * rows[2 * k + p][2 * m + q] for p in range(2) for q in range(2))
                for m in range(half)
            ]
            for k in range(half)
        ]
    return coefs


def total(value):
    return jnp.sum(jnp.sum(value, axis=0, keepdims=True), axis=1, keepdims=True)


def as_tile(sums, places):
    row = lax.broadcasted_iota(jnp.int32, (8, 128), 0)
    col = lax.broadcasted_iota(jnp.int32, (8, 128), 1)
    tile = jnp.zeros((8, 128), F32)
    for (i, j), value in sums.items():
        for a, b in [(i, j), (j, i)]:
            tile = jnp.where((row == places[a]) & (col == places[b]), value, tile)
    return tile


def from_tile(tile, count):
    col = lax.broadcasted_iota(jnp.int32, (8, 128), 1)
    columns = [jnp.sum(jnp.where(col == j, tile, 0.0), axis=1, keepdims=True) for j in range(count)]
    return [[columns[j][i : i + 1] for j in range(count)] for i in range(count)]


def ordered_coefs(tile, places):
    count = len(places)
    coefs = tree_coefs(from_tile(tile, count))
    chosen = [sum(jnp.where(place == i, coefs[i], 0.0) for i in range(count)) for place in places]
    return [value[0, 0] for value in chosen]


VMEM = pl.BlockSpec(memory_space=pltpu.VMEM)
SMEM = pl.BlockSpec(memory_space=pltpu.SMEM)
PARAMS = pltpu.CompilerParams(vmem_limit_bytes=16 * 2**20)
TILE = jax.ShapeDtypeStruct((8, 128), F32)


def grad_of(us, cs, scale):
    u, c = jnp.concatenate(us, 0), jnp.concatenate(cs, 0)
    grad = lax.dot_general(u, c, (((0,), (0,)), ((), ())), preferred_element_type=F32)
    return (grad * scale).astype(BF16)


def gram_kernel(pairs, shifts, count, at, *refs):
    *parts, out = refs
    before = parts.pop() if len(parts) > len(shifts) else None
    rows, width = parts[0].shape
    parts = dict(zip(shifts, parts))
    full = width // 128 * 128

    def step(k, sums):
        head, tail = list(sums[0]), list(sums[1])
        here = pl.ds(pl.multiple_of(k * 16, 16), 16)
        for start in range(0, width, 128):
            x = {d: ref[here, start : min(start + 128, width)].astype(F32) for d, ref in parts.items()}
            bag = tail if start == full else head
            for n, (i, j) in enumerate(pairs):
                prod = x[i] * x[j]
                bag[n] = bag[n] + (prod[:8] + prod[8:])
        return tuple(head), tuple(tail)

    if rows % 16 == 0:
        zeros = tuple(jnp.zeros((8, 128), F32) for _ in pairs)
        short = tuple(jnp.zeros((8, width - full), F32) for _ in pairs)
        head, tail = lax.fori_loop(0, rows // 16, step, (zeros, short), unroll=2)
        sums = {p: total(h) + total(t) for p, h, t in zip(pairs, head, tail)}
    else:
        x = {d: ref[...].astype(F32) for d, ref in parts.items()}
        sums = {(i, j): total(x[i] * x[j]) for i, j in pairs}
    tile = as_tile(sums, [lax.rem(at[0] - d + count, count) for d in range(count)])
    out[...] = tile if before is None else tile + before[...]


def gram_call(parts, at, pairs, count, before=None):
    shifts = [d for d in parts if any(d in pair for pair in pairs)]
    args = [parts[d] for d in shifts] + ([] if before is None else [before])
    return pl.pallas_call(
        lambda *refs: gram_kernel(pairs, shifts, count, *refs),
        out_shape=TILE,
        in_specs=[SMEM] + [VMEM] * len(args),
        out_specs=VMEM,
        compiler_params=PARAMS,
        name="gram%d_%d" % (count, len(pairs)),
    )(at, *args)


def mix_x_kernel(shifts, at, tile, own, other, *outs):
    coefs = ordered_coefs(tile[...], [at[0], 1 - at[0]])
    rows = outs[0].shape[0]
    for shift, out in zip(shifts, outs):
        base = lax.rem(at[1] + shift, 4) * rows

        def step(k, _):
            here = pl.ds(pl.multiple_of(base + k * 32, 16), 32)
            mixed = coefs[0] * own[here].astype(F32) + coefs[1] * other[here].astype(F32)
            out[pl.ds(pl.multiple_of(k * 32, 32), 32)] = mixed.astype(BF16)
            return 0

        lax.fori_loop(0, rows // 32, step, 0)


def mix_x_call(shifts, at, tile, own, other):
    piece = jax.ShapeDtypeStruct((own.shape[0] // 4, own.shape[1]), BF16)
    return pl.pallas_call(
        lambda *refs: mix_x_kernel(shifts, *refs),
        out_shape=(piece,) * len(shifts),
        in_specs=[SMEM] + [VMEM] * 3,
        out_specs=(VMEM,) * len(shifts),
        compiler_params=PARAMS,
        name="mix_x%d" % len(shifts),
    )(at, tile, own, other)


def mix_y_kernel(at, tile, *refs):
    parts, outs, hold = refs[:4], refs[4:12], refs[12]
    coefs = ordered_coefs(tile[...], [lax.rem(at[0] - d + 4, 4) for d in range(4)])
    rows = outs[0].shape[0]
    mixed = sum(c * ref[...].astype(F32) for c, ref in zip(coefs, parts))
    for k in range(8):
        hold[k] = mixed[k * rows : (k + 1) * rows]
    for d in range(8):
        outs[d][...] = hold[lax.rem(at[1] + d, 8)].astype(BF16)


def mix_y_call(at, tile, parts):
    rows, width = parts[0].shape
    return pl.pallas_call(
        mix_y_kernel,
        out_shape=tuple(jax.ShapeDtypeStruct((rows // 8, width), BF16) for _ in range(8)),
        in_specs=[SMEM] + [VMEM] * 5,
        out_specs=(VMEM,) * 8,
        scratch_shapes=[pltpu.VMEM((8, rows // 8, width), F32)],
        compiler_params=PARAMS,
        name="mix_y",
    )(at, tile, *parts)


def mix_z_kernel(shifts, at, tile, *refs):
    parts, out = refs[:8], refs[8]
    coefs = ordered_coefs(tile[...], [lax.rem(at[0] - d + 8, 8) for d in shifts])
    out[...] = sum(c * ref[...].astype(F32) for c, ref in zip(coefs, parts)).astype(BF16)


def mix_z_call(at, tile, parts):
    return pl.pallas_call(
        lambda *refs: mix_z_kernel(list(parts), *refs),
        out_shape=jax.ShapeDtypeStruct(parts[0].shape, BF16),
        in_specs=[SMEM] + [VMEM] * 9,
        out_specs=VMEM,
        compiler_params=PARAMS,
        name="mix_z",
    )(at, tile, *parts.values())


def tied(value, *after):
    return lax.optimization_barrier((value,) + after)[0]


def on_device(context, upstream, weight):
    tokens = context.shape[0]
    half = context.shape[1] // 2
    quarter = half // 2
    z, y = lax.axis_index("z"), lax.axis_index("y")
    xl, xh, core = lax.axis_index("xl"), lax.axis_index("xh"), lax.axis_index("c")
    d_half = xl ^ xh
    pick = lambda flag, a, b: jnp.where(flag == 1, b, a)

    u0, u1 = upstream[:, :half], upstream[:, half:]
    u_own, u_rest = pick(d_half, u0, u1), pick(d_half, u1, u0)
    c0, c1 = context[:, :half], context[:, half:]
    c_own, c_rest = pick(xh, c0, c1), pick(xh, c1, c0)
    u_sib = send(u_rest, SIB)
    c_mate = send(c_rest, MATE)
    us_rest = [u_rest, send(u_rest, CHIP)]
    c_own, u_own = lax.optimization_barrier((c_own, u_own, us_rest[1]))[:2]
    c_sib = send(c_own, SIB)
    u_mate = send(u_own, MATE)
    c_opp = send(c_mate, SIB)
    u_opp = send(u_sib, MATE)

    def both_cores(value):
        return [value, send(value, CHIP)]

    def quarters(value):
        keep = pick(core, value[:, :quarter], value[:, quarter:])
        give = pick(core, value[:, quarter:], value[:, :quarter])
        return [keep, send(give, CHIP)]

    at = lambda *values: jnp.stack([v.astype(jnp.int32) for v in values])
    at_x, at_yz, at_z = at(xl, y), at(y, z), at(z)
    scale = 1.0 / (4 * tokens)
    us_own, us_mate = both_cores(u_own), both_cores(u_mate)
    other = grad_of(both_cores(u_sib) + us_mate, quarters(c_sib) + quarters(c_mate), scale)
    sums = gram_call({1: other}, at_x, [(1, 1)], 2)
    u_opp, c_opp, sums = lax.optimization_barrier((u_opp, c_opp, sums))
    own = grad_of(us_own + both_cores(u_opp), quarters(c_own) + quarters(c_opp), scale)
    sums = sum_x(gram_call({0: own, 1: other}, at_x, [(0, 0), (0, 1)], 2, sums))

    pieces = dict(zip((1, 3, 2), mix_x_call((1, 3, 2), at_x, sums, own, other)))
    parts = {d: send(pieces[d], Y_SHIFT[d]) for d in (1, 3, 2)}
    u_mate_rest = send(tied(u_rest, pieces[2]), MATE)
    parts[0] = mix_x_call((0,), at_x, tied(sums, u_mate_rest), own, other)[0]

    us_own = [tied(u, u_mate_rest) for u in us_own]
    u_a = jnp.concatenate(us_own + us_mate, 0)
    u_b = jnp.concatenate(us_rest + both_cores(u_mate_rest), 0)
    wide = jnp.concatenate([pick(d_half, u_a, u_b), pick(d_half, u_b, u_a)], 1)
    back = lax.dot_general(wide, weight, (((1,), (1,)), ((), ())), preferred_element_type=F32).astype(BF16)

    def token_rows(value):
        mine, theirs = value[:tokens], send(value[tokens:], CHIP)
        return jnp.concatenate([pick(core, mine, theirs), pick(core, theirs, mine)], 1)

    near = token_rows(back[: 2 * tokens])
    far = send(token_rows(back[2 * tokens :]), MATE)
    near, far, parts[2] = lax.optimization_barrier((near, far, parts[2]))

    parts = {d: parts[d] for d in (0, 1, 3, 2)}
    sums = gram_call(parts, at_yz, [(0, 0), (1, 1), (3, 3), (0, 1), (0, 3), (1, 3)], 4)
    sums = gram_call(parts, at_yz, [(0, 2), (1, 2), (2, 3), (2, 2)], 4, sums)
    sums = sum_x(sum_y(sums))
    pieces = mix_y_call(at_yz, sums, [parts[d] for d in range(4)])

    near_first = (0, 1, 7, 2, 6, 3, 5, 4)
    parts = {d: send(pieces[d], Z_SHIFT[d]) if d else pieces[0] for d in near_first}
    d_context = jnp.concatenate([pick(xh, near, far), pick(xh, far, near)], 1)
    d_context, parts[1] = lax.optimization_barrier((d_context, parts[1]))
    sums = gram_call(parts, at_z, [(i, j) for i in range(8) for j in range(i, 8)], 8)
    sums = sum_z(sum_x(sum_y(sums)))
    vector = mix_z_call(at_z, sums, parts)
    return d_context, send(vector, FINAL).T


def solution(mesh):
    fine = Mesh(mesh.devices.reshape(SIZES), AXES)
    return jax.shard_map(
        on_device,
        mesh=fine,
        in_specs=(P(AXES, None), P(AXES, None), P(("xh", "c"), None)),
        out_specs=(P(AXES, None), P(("xh", "c"), ("z", "y", "xl"))),
        check_vma=False,
    )
```

```python
import jax
import jax.numpy as jnp
import numpy as np
from jax import lax
from jax.experimental import pallas as pl
from jax.experimental.pallas import tpu as pltpu
from jax.sharding import Mesh
from jax.sharding import PartitionSpec as P

AXES = ("z", "y", "xl", "xh", "c")
SIZES = (8, 4, 2, 2, 2)
BF16 = jnp.bfloat16
F32 = jnp.float32


def routes(where_to):
    pairs = []
    for source, (z, y, xl, xh, c) in enumerate(np.ndindex(*SIZES)):
        z2, y2, x2, c2 = where_to(z, y, 2 * xh + xl, c)
        place = (z2 % 8, y2 % 4, x2 & 1, x2 >> 1, c2)
        pairs.append((source, int(np.ravel_multi_index(place, SIZES))))
    return pairs


SIB = routes(lambda z, y, x, c: (z, y, x ^ 1, c))
MATE = routes(lambda z, y, x, c: (z, y, 3 - x, c))
OPP = routes(lambda z, y, x, c: (z, y, x ^ 2, c))
CHIP = routes(lambda z, y, x, c: (z, y, x, 1 - c))
Y_SHIFT = [routes(lambda z, y, x, c, d=d: (z, y + d, x, c)) for d in range(4)]
Z_SHIFT = [routes(lambda z, y, x, c, d=d: (z + d, y, x, c)) for d in range(8)]
Z_SPLIT = [routes(lambda z, y, x, c, d=d: (z - d if c else z + d, y, x, c)) for d in (1, 2, 3)]
Z_SPLIT.append([(a, b) for a, b in Z_SHIFT[4] if a % 2])


def final_place(z, y, x, c):
    block = ((x & 1) ^ (x >> 1)) * 32 + y * 8 + z
    return (block >> 3, (block >> 1) & 3, (x & 2) | (block & 1), c)


FINAL = routes(final_place)


def send(value, pairs):
    return lax.ppermute(value, AXES, pairs)


def sum_x(s):
    s = s + send(s, CHIP)
    return s + send(s, SIB) + send(s, MATE) + send(s, OPP)


def sum_y(s):
    return s + send(s, Y_SHIFT[1]) + send(s, Y_SHIFT[2]) + send(s, Y_SHIFT[3])


def sum_z(s):
    own = jnp.where(lax.axis_index("c") == 0, s, 0.0)
    s = own + sum(send(s, pairs) for pairs in Z_SPLIT)
    return s + send(s, CHIP)


def tree_coefs(rows):
    count = len(rows)
    coefs = [1.0] * count
    while len(rows) > 1:
        half = len(rows) // 2
        span = count // len(rows)
        pair = []
        for k in range(half):
            cross = rows[2 * k][2 * k + 1]
            pair.append([1.0 - cross / (2.0 * rows[2 * k + p][2 * k + p]) for p in range(2)])
        coefs = [coefs[i] * pair[i // (2 * span)][(i // span) % 2] for i in range(count)]
        rows = [
            [
                sum(pair[k][p] * pair[m][q] * rows[2 * k + p][2 * m + q] for p in range(2) for q in range(2))
                for m in range(half)
            ]
            for k in range(half)
        ]
    return coefs


def total(value):
    return jnp.sum(jnp.sum(value, axis=0, keepdims=True), axis=1, keepdims=True)


def as_tile(sums, places):
    row = lax.broadcasted_iota(jnp.int32, (8, 128), 0)
    col = lax.broadcasted_iota(jnp.int32, (8, 128), 1)
    tile = jnp.zeros((8, 128), F32)
    for (i, j), value in sums.items():
        for a, b in [(i, j), (j, i)]:
            tile = jnp.where((row == places[a]) & (col == places[b]), value, tile)
    return tile


def from_tile(tile, count):
    col = lax.broadcasted_iota(jnp.int32, (8, 128), 1)
    columns = [jnp.sum(jnp.where(col == j, tile, 0.0), axis=1, keepdims=True) for j in range(count)]
    return [[columns[j][i : i + 1] for j in range(count)] for i in range(count)]


def ordered_coefs(tile, places):
    count = len(places)
    coefs = tree_coefs(from_tile(tile, count))
    chosen = [sum(jnp.where(place == i, coefs[i], 0.0) for i in range(count)) for place in places]
    return [value[0, 0] for value in chosen]


VMEM = pl.BlockSpec(memory_space=pltpu.VMEM)
SMEM = pl.BlockSpec(memory_space=pltpu.SMEM)
PARAMS = pltpu.CompilerParams(vmem_limit_bytes=10 * 2**20)
TILE = jax.ShapeDtypeStruct((8, 128), F32)


def grad_of(us, cs, scale):
    u, c = jnp.concatenate(us, 0), jnp.concatenate(cs, 0)
    grad = lax.dot_general(u, c, (((0,), (0,)), ((), ())), preferred_element_type=F32)
    return (grad * scale).astype(BF16)


def gram_kernel(pairs, shifts, count, at, *refs):
    *parts, out = refs
    before = parts.pop() if len(parts) > len(shifts) else None
    rows, width = parts[0].shape
    parts = dict(zip(shifts, parts))
    full = width // 128 * 128

    def step(k, sums):
        head, tail = list(sums[0]), list(sums[1])
        here = pl.ds(pl.multiple_of(k * 16, 16), 16)
        for start in range(0, width, 128):
            x = {d: ref[here, start : min(start + 128, width)].astype(F32) for d, ref in parts.items()}
            bag = tail if start == full else head
            for n, (i, j) in enumerate(pairs):
                prod = x[i] * x[j]
                bag[n] = bag[n] + (prod[:8] + prod[8:])
        return tuple(head), tuple(tail)

    if rows % 16 == 0:
        zeros = tuple(jnp.zeros((8, 128), F32) for _ in pairs)
        short = tuple(jnp.zeros((8, width - full), F32) for _ in pairs)
        head, tail = lax.fori_loop(0, rows // 16, step, (zeros, short), unroll=2)
        sums = {p: total(h) + total(t) for p, h, t in zip(pairs, head, tail)}
    else:
        x = {d: ref[...].astype(F32) for d, ref in parts.items()}
        sums = {(i, j): total(x[i] * x[j]) for i, j in pairs}
    tile = as_tile(sums, [lax.rem(at[0] - d + count, count) for d in range(count)])
    out[...] = tile if before is None else tile + before[...]


def gram_call(parts, at, pairs, count, before=None):
    shifts = [d for d in parts if any(d in pair for pair in pairs)]
    args = [parts[d] for d in shifts] + ([] if before is None else [before])
    return pl.pallas_call(
        lambda *refs: gram_kernel(pairs, shifts, count, *refs),
        out_shape=TILE,
        in_specs=[SMEM] + [VMEM] * len(args),
        out_specs=VMEM,
        compiler_params=PARAMS,
        name="gram%d_%d" % (count, len(pairs)),
    )(at, *args)


def mix_x_kernel(shifts, at, tile, own, other, *outs):
    coefs = ordered_coefs(tile[...], [at[0], 1 - at[0]])
    rows = outs[0].shape[0]
    for shift, out in zip(shifts, outs):
        base = lax.rem(at[1] + shift, 4) * rows

        def step(k, _):
            here = pl.ds(pl.multiple_of(base + k * 32, 16), 32)
            mixed = coefs[0] * own[here].astype(F32) + coefs[1] * other[here].astype(F32)
            out[pl.ds(pl.multiple_of(k * 32, 32), 32)] = mixed.astype(BF16)
            return 0

        lax.fori_loop(0, rows // 32, step, 0)


def mix_x_call(shifts, at, tile, own, other):
    piece = jax.ShapeDtypeStruct((own.shape[0] // 4, own.shape[1]), BF16)
    return pl.pallas_call(
        lambda *refs: mix_x_kernel(shifts, *refs),
        out_shape=(piece,) * len(shifts),
        in_specs=[SMEM] + [VMEM] * 3,
        out_specs=(VMEM,) * len(shifts),
        compiler_params=PARAMS,
        name="mix_x%d" % len(shifts),
    )(at, tile, own, other)


def mix_y_kernel(at, tile, *refs):
    parts, outs, hold = refs[:4], refs[4:12], refs[12]
    coefs = ordered_coefs(tile[...], [lax.rem(at[0] - d + 4, 4) for d in range(4)])
    rows = outs[0].shape[0]
    mixed = sum(c * ref[...].astype(F32) for c, ref in zip(coefs, parts))
    for k in range(8):
        hold[k] = mixed[k * rows : (k + 1) * rows]
    for d in range(8):
        outs[d][...] = hold[lax.rem(at[1] + d, 8)].astype(BF16)


def mix_y_call(at, tile, parts):
    rows, width = parts[0].shape
    return pl.pallas_call(
        mix_y_kernel,
        out_shape=tuple(jax.ShapeDtypeStruct((rows // 8, width), BF16) for _ in range(8)),
        in_specs=[SMEM] + [VMEM] * 5,
        out_specs=(VMEM,) * 8,
        scratch_shapes=[pltpu.VMEM((8, rows // 8, width), F32)],
        compiler_params=PARAMS,
        name="mix_y",
    )(at, tile, *parts)


def mix_z_kernel(shifts, at, tile, *refs):
    parts, out = refs[:8], refs[8]
    coefs = ordered_coefs(tile[...], [lax.rem(at[0] - d + 8, 8) for d in shifts])
    out[...] = sum(c * ref[...].astype(F32) for c, ref in zip(coefs, parts)).astype(BF16)


def mix_z_call(at, tile, parts):
    return pl.pallas_call(
        lambda *refs: mix_z_kernel(list(parts), *refs),
        out_shape=jax.ShapeDtypeStruct(parts[0].shape, BF16),
        in_specs=[SMEM] + [VMEM] * 9,
        out_specs=VMEM,
        compiler_params=PARAMS,
        name="mix_z",
    )(at, tile, *parts.values())


def on_device(context, upstream, weight):
    tokens = context.shape[0]
    half = context.shape[1] // 2
    quarter = half // 2
    z, y = lax.axis_index("z"), lax.axis_index("y")
    xl, xh, core = lax.axis_index("xl"), lax.axis_index("xh"), lax.axis_index("c")
    d_half = xl ^ xh
    pick = lambda flag, a, b: jnp.where(flag == 1, b, a)

    u0, u1 = upstream[:, :half], upstream[:, half:]
    u_own, u_rest = pick(d_half, u0, u1), pick(d_half, u1, u0)
    c0, c1 = context[:, :half], context[:, half:]
    c_own, c_rest = pick(xh, c0, c1), pick(xh, c1, c0)
    u_sib = send(u_rest, SIB)
    c_mate = send(c_rest, MATE)
    us_rest = [u_rest, send(u_rest, CHIP)]
    c_own, u_own = lax.optimization_barrier((c_own, u_own, us_rest[1]))[:2]
    c_sib = send(c_own, SIB)
    u_mate = send(u_own, MATE)
    c_opp = send(c_mate, SIB)
    u_opp = send(u_sib, MATE)

    def both_cores(value):
        return [value, send(value, CHIP)]

    def quarters(value):
        keep = pick(core, value[:, :quarter], value[:, quarter:])
        give = pick(core, value[:, quarter:], value[:, :quarter])
        return [keep, send(give, CHIP)]

    at = lambda *values: jnp.stack([v.astype(jnp.int32) for v in values])
    at_x, at_yz, at_z = at(xl, y), at(y, z), at(z)
    scale = 1.0 / (4 * tokens)
    us_own, us_mate = both_cores(u_own), both_cores(u_mate)
    other = grad_of(both_cores(u_sib) + us_mate, quarters(c_sib) + quarters(c_mate), scale)
    c_opp, u_opp, u_late, other = lax.optimization_barrier((c_opp, u_opp, u_rest, other))
    u_mate_rest = send(u_late, MATE)
    sums = gram_call({1: other}, at_x, [(1, 1)], 2)
    own = grad_of(us_own + both_cores(u_opp), quarters(c_own) + quarters(c_opp), scale)
    sums = sum_x(gram_call({0: own, 1: other}, at_x, [(0, 0), (0, 1)], 2, sums))

    pieces = dict(zip((1, 3, 2), mix_x_call((1, 3, 2), at_x, sums, own, other)))
    parts = {d: send(pieces[d], Y_SHIFT[d]) for d in (1, 3, 2)}
    parts[0] = mix_x_call((0,), at_x, sums, own, other)[0]

    u_a = jnp.concatenate(us_own + us_mate, 0)
    u_b = jnp.concatenate(us_rest + both_cores(u_mate_rest), 0)
    wide = jnp.concatenate([pick(d_half, u_a, u_b), pick(d_half, u_b, u_a)], 1)
    back = lax.dot_general(wide, weight, (((1,), (1,)), ((), ())), preferred_element_type=F32).astype(BF16)

    at_yz, back = lax.optimization_barrier((at_yz, back))

    def token_rows(value):
        mine, theirs = value[:tokens], send(value[tokens:], CHIP)
        return jnp.concatenate([pick(core, mine, theirs), pick(core, theirs, mine)], 1)

    near = token_rows(back[: 2 * tokens])
    far = send(token_rows(back[2 * tokens :]), MATE)

    parts = {d: parts[d] for d in (0, 1, 3, 2)}
    sums = gram_call(parts, at_yz, [(0, 0), (1, 1), (3, 3), (0, 1), (0, 3), (1, 3)], 4)
    sums = gram_call(parts, at_yz, [(0, 2), (1, 2), (2, 3), (2, 2)], 4, sums)
    sums = sum_x(sum_y(sums))
    pieces = mix_y_call(at_yz, sums, [parts[d] for d in range(4)])

    near_first = (0, 1, 7, 2, 6, 3, 5, 4)
    parts = {d: send(pieces[d], Z_SHIFT[d]) if d else pieces[0] for d in near_first}
    d_context = jnp.concatenate([pick(xh, near, far), pick(xh, far, near)], 1)
    at_z, d_context = lax.optimization_barrier((at_z, d_context))
    sums = gram_call(parts, at_z, [(i, j) for i in range(8) for j in range(i, 8)], 8)
    sums = sum_z(sum_x(sum_y(sums)))
    vector = mix_z_call(at_z, sums, parts)
    return d_context, send(vector, FINAL).T


def solution(mesh):
    fine = Mesh(mesh.devices.reshape(SIZES), AXES)
    return jax.shard_map(
        on_device,
        mesh=fine,
        in_specs=(P(AXES, None), P(AXES, None), P(("xh", "c"), None)),
        out_specs=(P(AXES, None), P(("xh", "c"), ("z", "y", "xl"))),
        check_vma=False,
    )
```

```python
import jax
import jax.numpy as jnp
import numpy as np
from jax import lax
from jax.experimental import pallas as pl
from jax.experimental.pallas import tpu as pltpu
from jax.sharding import Mesh
from jax.sharding import PartitionSpec as P

AXES = ("z", "y", "xl", "xh", "c")
SIZES = (8, 4, 2, 2, 2)
BF16 = jnp.bfloat16
F32 = jnp.float32


def routes(where_to):
    pairs = []
    for source, (z, y, xl, xh, c) in enumerate(np.ndindex(*SIZES)):
        z2, y2, x2, c2 = where_to(z, y, 2 * xh + xl, c)
        place = (z2 % 8, y2 % 4, x2 & 1, x2 >> 1, c2)
        pairs.append((source, int(np.ravel_multi_index(place, SIZES))))
    return pairs


SIB = routes(lambda z, y, x, c: (z, y, x ^ 1, c))
MATE = routes(lambda z, y, x, c: (z, y, 3 - x, c))
OPP = routes(lambda z, y, x, c: (z, y, x ^ 2, c))
CHIP = routes(lambda z, y, x, c: (z, y, x, 1 - c))
Y_SHIFT = [routes(lambda z, y, x, c, d=d: (z, y + d, x, c)) for d in range(4)]
Z_SHIFT = [routes(lambda z, y, x, c, d=d: (z + d, y, x, c)) for d in range(8)]
Z_SPLIT = [routes(lambda z, y, x, c, d=d: (z - d if c else z + d, y, x, c)) for d in (1, 2, 3)]
Z_SPLIT.append([(a, b) for a, b in Z_SHIFT[4] if a % 2])


def final_place(z, y, x, c):
    block = ((x & 1) ^ (x >> 1)) * 32 + y * 8 + z
    return (block >> 3, (block >> 1) & 3, (x & 2) | (block & 1), c)


FINAL = routes(final_place)


def send(value, pairs):
    return lax.ppermute(value, AXES, pairs)


def sum_x(s):
    s = s + send(s, CHIP)
    return s + send(s, SIB) + send(s, MATE) + send(s, OPP)


def sum_y(s):
    return s + send(s, Y_SHIFT[1]) + send(s, Y_SHIFT[2]) + send(s, Y_SHIFT[3])


def sum_z(s):
    own = jnp.where(lax.axis_index("c") == 0, s, 0.0)
    s = own + sum(send(s, pairs) for pairs in Z_SPLIT)
    return s + send(s, CHIP)


def tree_coefs(rows):
    count = len(rows)
    coefs = [1.0] * count
    while len(rows) > 1:
        half = len(rows) // 2
        span = count // len(rows)
        pair = []
        for k in range(half):
            cross = rows[2 * k][2 * k + 1]
            pair.append([1.0 - cross / (2.0 * rows[2 * k + p][2 * k + p]) for p in range(2)])
        coefs = [coefs[i] * pair[i // (2 * span)][(i // span) % 2] for i in range(count)]
        rows = [
            [
                sum(pair[k][p] * pair[m][q] * rows[2 * k + p][2 * m + q] for p in range(2) for q in range(2))
                for m in range(half)
            ]
            for k in range(half)
        ]
    return coefs


def total(value):
    return jnp.sum(jnp.sum(value, axis=0, keepdims=True), axis=1, keepdims=True)


def as_tile(sums, places):
    row = lax.broadcasted_iota(jnp.int32, (8, 128), 0)
    col = lax.broadcasted_iota(jnp.int32, (8, 128), 1)
    tile = jnp.zeros((8, 128), F32)
    for (i, j), value in sums.items():
        for a, b in [(i, j), (j, i)]:
            tile = jnp.where((row == places[a]) & (col == places[b]), value, tile)
    return tile


def from_tile(tile, count):
    col = lax.broadcasted_iota(jnp.int32, (8, 128), 1)
    columns = [jnp.sum(jnp.where(col == j, tile, 0.0), axis=1, keepdims=True) for j in range(count)]
    return [[columns[j][i : i + 1] for j in range(count)] for i in range(count)]


def ordered_coefs(tile, places):
    count = len(places)
    coefs = tree_coefs(from_tile(tile, count))
    chosen = [sum(jnp.where(place == i, coefs[i], 0.0) for i in range(count)) for place in places]
    return [value[0, 0] for value in chosen]


VMEM = pl.BlockSpec(memory_space=pltpu.VMEM)
SMEM = pl.BlockSpec(memory_space=pltpu.SMEM)
PARAMS = pltpu.CompilerParams(vmem_limit_bytes=10 * 2**20)
TILE = jax.ShapeDtypeStruct((8, 128), F32)


def grad_of(us, cs, scale):
    u, c = jnp.concatenate(us, 0), jnp.concatenate(cs, 0)
    grad = lax.dot_general(u, c, (((0,), (0,)), ((), ())), preferred_element_type=F32)
    return (grad * scale).astype(BF16)


def gram_kernel(pairs, shifts, count, at, *refs):
    *parts, out = refs
    before = parts.pop() if len(parts) > len(shifts) else None
    rows, width = parts[0].shape
    parts = dict(zip(shifts, parts))
    full = width // 128 * 128

    def step(k, sums):
        head, tail = list(sums[0]), list(sums[1])
        here = pl.ds(pl.multiple_of(k * 16, 16), 16)
        for start in range(0, width, 128):
            x = {d: ref[here, start : min(start + 128, width)].astype(F32) for d, ref in parts.items()}
            bag = tail if start == full else head
            for n, (i, j) in enumerate(pairs):
                prod = x[i] * x[j]
                bag[n] = bag[n] + (prod[:8] + prod[8:])
        return tuple(head), tuple(tail)

    if rows % 16 == 0:
        zeros = tuple(jnp.zeros((8, 128), F32) for _ in pairs)
        short = tuple(jnp.zeros((8, width - full), F32) for _ in pairs)
        head, tail = lax.fori_loop(0, rows // 16, step, (zeros, short), unroll=2)
        sums = {p: total(h) + total(t) for p, h, t in zip(pairs, head, tail)}
    else:
        x = {d: ref[...].astype(F32) for d, ref in parts.items()}
        sums = {(i, j): total(x[i] * x[j]) for i, j in pairs}
    tile = as_tile(sums, [lax.rem(at[0] - d + count, count) for d in range(count)])
    out[...] = tile if before is None else tile + before[...]


def gram_call(parts, at, pairs, count, before=None):
    shifts = [d for d in parts if any(d in pair for pair in pairs)]
    args = [parts[d] for d in shifts] + ([] if before is None else [before])
    return pl.pallas_call(
        lambda *refs: gram_kernel(pairs, shifts, count, *refs),
        out_shape=TILE,
        in_specs=[SMEM] + [VMEM] * len(args),
        out_specs=VMEM,
        compiler_params=PARAMS,
        name="gram%d_%d" % (count, len(pairs)),
    )(at, *args)


def mix_x_kernel(shifts, at, tile, own, other, *outs):
    coefs = ordered_coefs(tile[...], [at[0], 1 - at[0]])
    rows = outs[0].shape[0]
    for shift, out in zip(shifts, outs):
        base = lax.rem(at[1] + shift, 4) * rows

        def step(k, _):
            here = pl.ds(pl.multiple_of(base + k * 32, 16), 32)
            mixed = coefs[0] * own[here].astype(F32) + coefs[1] * other[here].astype(F32)
            out[pl.ds(pl.multiple_of(k * 32, 32), 32)] = mixed.astype(BF16)
            return 0

        lax.fori_loop(0, rows // 32, step, 0)


def mix_x_call(shifts, at, tile, own, other):
    piece = jax.ShapeDtypeStruct((own.shape[0] // 4, own.shape[1]), BF16)
    return pl.pallas_call(
        lambda *refs: mix_x_kernel(shifts, *refs),
        out_shape=(piece,) * len(shifts),
        in_specs=[SMEM] + [VMEM] * 3,
        out_specs=(VMEM,) * len(shifts),
        compiler_params=PARAMS,
        name="mix_x%d" % len(shifts),
    )(at, tile, own, other)


def mix_y_kernel(at, tile, *refs):
    parts, outs, hold = refs[:4], refs[4:12], refs[12]
    coefs = ordered_coefs(tile[...], [lax.rem(at[0] - d + 4, 4) for d in range(4)])
    rows = outs[0].shape[0]
    mixed = sum(c * ref[...].astype(F32) for c, ref in zip(coefs, parts))
    for k in range(8):
        hold[k] = mixed[k * rows : (k + 1) * rows]
    for d in range(8):
        outs[d][...] = hold[lax.rem(at[1] + d, 8)].astype(BF16)


def mix_y_call(at, tile, parts):
    rows, width = parts[0].shape
    return pl.pallas_call(
        mix_y_kernel,
        out_shape=tuple(jax.ShapeDtypeStruct((rows // 8, width), BF16) for _ in range(8)),
        in_specs=[SMEM] + [VMEM] * 5,
        out_specs=(VMEM,) * 8,
        scratch_shapes=[pltpu.VMEM((8, rows // 8, width), F32)],
        compiler_params=PARAMS,
        name="mix_y",
    )(at, tile, *parts)


def mix_z_kernel(shifts, at, tile, *refs):
    parts, out = refs[:8], refs[8]
    coefs = ordered_coefs(tile[...], [lax.rem(at[0] - d + 8, 8) for d in shifts])
    out[...] = sum(c * ref[...].astype(F32) for c, ref in zip(coefs, parts)).astype(BF16)


def mix_z_call(at, tile, parts):
    return pl.pallas_call(
        lambda *refs: mix_z_kernel(list(parts), *refs),
        out_shape=jax.ShapeDtypeStruct(parts[0].shape, BF16),
        in_specs=[SMEM] + [VMEM] * 9,
        out_specs=VMEM,
        compiler_params=PARAMS,
        name="mix_z",
    )(at, tile, *parts.values())


def tied(value, *after):
    return lax.optimization_barrier((value,) + after)[0]


def on_device(context, upstream, weight):
    tokens = context.shape[0]
    half = context.shape[1] // 2
    quarter = half // 2
    z, y = lax.axis_index("z"), lax.axis_index("y")
    xl, xh, core = lax.axis_index("xl"), lax.axis_index("xh"), lax.axis_index("c")
    d_half = xl ^ xh
    pick = lambda flag, a, b: jnp.where(flag == 1, b, a)

    u0, u1 = upstream[:, :half], upstream[:, half:]
    u_own, u_rest = pick(d_half, u0, u1), pick(d_half, u1, u0)
    c0, c1 = context[:, :half], context[:, half:]
    c_own, c_rest = pick(xh, c0, c1), pick(xh, c1, c0)
    u_sib = send(u_rest, SIB)
    c_mate = send(c_rest, MATE)
    us_rest = [u_rest, send(u_rest, CHIP)]
    c_own, u_own = lax.optimization_barrier((c_own, u_own, us_rest[1]))[:2]
    c_sib = send(c_own, SIB)
    u_mate = send(u_own, MATE)
    c_opp = send(c_mate, SIB)
    u_opp = send(u_sib, MATE)

    def both_cores(value):
        return [value, send(value, CHIP)]

    def quarters(value):
        keep = pick(core, value[:, :quarter], value[:, quarter:])
        give = pick(core, value[:, quarter:], value[:, :quarter])
        return [keep, send(give, CHIP)]

    at = lambda *values: jnp.stack([v.astype(jnp.int32) for v in values])
    at_x, at_yz, at_z = at(xl, y), at(y, z), at(z)
    scale = 1.0 / (4 * tokens)
    us_own, us_mate = both_cores(u_own), both_cores(u_mate)
    other = grad_of(both_cores(u_sib) + us_mate, quarters(c_sib) + quarters(c_mate), scale)
    sums = gram_call({1: other}, at_x, [(1, 1)], 2)
    u_opp, c_opp, sums = lax.optimization_barrier((u_opp, c_opp, sums))
    own = grad_of(us_own + both_cores(u_opp), quarters(c_own) + quarters(c_opp), scale)
    sums = sum_x(gram_call({0: own, 1: other}, at_x, [(0, 0), (0, 1)], 2, sums))

    pieces = dict(zip((1, 3, 2), mix_x_call((1, 3, 2), at_x, sums, own, other)))
    parts = {d: send(pieces[d], Y_SHIFT[d]) for d in (1, 3, 2)}
    u_mate_rest = send(tied(u_rest, pieces[2]), MATE)
    parts[0] = mix_x_call((0,), at_x, tied(sums, u_mate_rest), own, other)[0]

    us_own = [tied(u, u_mate_rest) for u in us_own]
    u_a = jnp.concatenate(us_own + us_mate, 0)
    u_b = jnp.concatenate(us_rest + both_cores(u_mate_rest), 0)
    wide = jnp.concatenate([pick(d_half, u_a, u_b), pick(d_half, u_b, u_a)], 1)
    back = lax.dot_general(wide, weight, (((1,), (1,)), ((), ())), preferred_element_type=F32).astype(BF16)

    def token_rows(value):
        mine, theirs = value[:tokens], send(value[tokens:], CHIP)
        return jnp.concatenate([pick(core, mine, theirs), pick(core, theirs, mine)], 1)

    near = token_rows(back[: 2 * tokens])
    far = send(token_rows(back[2 * tokens :]), MATE)
    near, far, parts[2] = lax.optimization_barrier((near, far, parts[2]))

    parts = {d: parts[d] for d in (0, 1, 3, 2)}
    sums = gram_call(parts, at_yz, [(0, 0), (1, 1), (3, 3), (0, 1), (0, 3), (1, 3)], 4)
    sums = gram_call(parts, at_yz, [(0, 2), (1, 2), (2, 3), (2, 2)], 4, sums)
    sums = sum_x(sum_y(sums))
    pieces = mix_y_call(at_yz, sums, [parts[d] for d in range(4)])

    near_first = (0, 1, 7, 2, 6, 3, 5, 4)
    parts = {d: send(pieces[d], Z_SHIFT[d]) if d else pieces[0] for d in near_first}
    d_context = jnp.concatenate([pick(xh, near, far), pick(xh, far, near)], 1)
    d_context, parts[1] = lax.optimization_barrier((d_context, parts[1]))
    sums = gram_call(parts, at_z, [(i, j) for i in range(8) for j in range(i, 8)], 8)
    sums = sum_z(sum_x(sum_y(sums)))
    vector = mix_z_call(at_z, sums, parts)
    return d_context, send(vector, FINAL).T


def solution(mesh):
    fine = Mesh(mesh.devices.reshape(SIZES), AXES)
    return jax.shard_map(
        on_device,
        mesh=fine,
        in_specs=(P(AXES, None), P(AXES, None), P(("xh", "c"), None)),
        out_specs=(P(AXES, None), P(("xh", "c"), ("z", "y", "xl"))),
        check_vma=False,
    )
```

```python
import jax
import jax.numpy as jnp
import numpy as np
from jax import lax
from jax.experimental import pallas as pl
from jax.experimental.pallas import tpu as pltpu
from jax.sharding import Mesh
from jax.sharding import PartitionSpec as P

AXES = ("z", "y", "xl", "xh", "c")
SIZES = (8, 4, 2, 2, 2)
BF16 = jnp.bfloat16
F32 = jnp.float32


def routes(where_to):
    pairs = []
    for source, (z, y, xl, xh, c) in enumerate(np.ndindex(*SIZES)):
        z2, y2, x2, c2 = where_to(z, y, 2 * xh + xl, c)
        place = (z2 % 8, y2 % 4, x2 & 1, x2 >> 1, c2)
        pairs.append((source, int(np.ravel_multi_index(place, SIZES))))
    return pairs


SIB = routes(lambda z, y, x, c: (z, y, x ^ 1, c))
MATE = routes(lambda z, y, x, c: (z, y, 3 - x, c))
OPP = routes(lambda z, y, x, c: (z, y, x ^ 2, c))
CHIP = routes(lambda z, y, x, c: (z, y, x, 1 - c))
Y_SHIFT = [routes(lambda z, y, x, c, d=d: (z, y + d, x, c)) for d in range(4)]
Z_SHIFT = [routes(lambda z, y, x, c, d=d: (z + d, y, x, c)) for d in range(8)]
Z_SPLIT = [routes(lambda z, y, x, c, d=d: (z - d if c else z + d, y, x, c)) for d in (1, 2, 3)]
Z_SPLIT.append([(a, b) for a, b in Z_SHIFT[4] if a % 2])


def final_place(z, y, x, c):
    block = ((x & 1) ^ (x >> 1)) * 32 + y * 8 + z
    return (block >> 3, (block >> 1) & 3, (x & 2) | (block & 1), c)


FINAL = routes(final_place)


def send(value, pairs):
    return lax.ppermute(value, AXES, pairs)


def sum_x(s):
    s = s + send(s, CHIP)
    return s + send(s, SIB) + send(s, MATE) + send(s, OPP)


def sum_y(s):
    return s + send(s, Y_SHIFT[1]) + send(s, Y_SHIFT[2]) + send(s, Y_SHIFT[3])


def sum_z(s):
    own = jnp.where(lax.axis_index("c") == 0, s, 0.0)
    s = own + sum(send(s, pairs) for pairs in Z_SPLIT)
    return s + send(s, CHIP)


def tree_coefs(rows):
    count = len(rows)
    coefs = [1.0] * count
    while len(rows) > 1:
        half = len(rows) // 2
        span = count // len(rows)
        pair = []
        for k in range(half):
            cross = rows[2 * k][2 * k + 1]
            pair.append([1.0 - cross / (2.0 * rows[2 * k + p][2 * k + p]) for p in range(2)])
        coefs = [coefs[i] * pair[i // (2 * span)][(i // span) % 2] for i in range(count)]
        rows = [
            [
                sum(pair[k][p] * pair[m][q] * rows[2 * k + p][2 * m + q] for p in range(2) for q in range(2))
                for m in range(half)
            ]
            for k in range(half)
        ]
    return coefs


def total(value):
    return jnp.sum(jnp.sum(value, axis=0, keepdims=True), axis=1, keepdims=True)


def as_tile(sums, places):
    row = lax.broadcasted_iota(jnp.int32, (8, 128), 0)
    col = lax.broadcasted_iota(jnp.int32, (8, 128), 1)
    tile = jnp.zeros((8, 128), F32)
    for (i, j), value in sums.items():
        for a, b in [(i, j), (j, i)]:
            tile = jnp.where((row == places[a]) & (col == places[b]), value, tile)
    return tile


def from_tile(tile, count):
    col = lax.broadcasted_iota(jnp.int32, (8, 128), 1)
    columns = [jnp.sum(jnp.where(col == j, tile, 0.0), axis=1, keepdims=True) for j in range(count)]
    return [[columns[j][i : i + 1] for j in range(count)] for i in range(count)]


def ordered_coefs(tile, places):
    count = len(places)
    coefs = tree_coefs(from_tile(tile, count))
    chosen = [sum(jnp.where(place == i, coefs[i], 0.0) for i in range(count)) for place in places]
    return [value[0, 0] for value in chosen]


VMEM = pl.BlockSpec(memory_space=pltpu.VMEM)
SMEM = pl.BlockSpec(memory_space=pltpu.SMEM)
PARAMS = pltpu.CompilerParams(vmem_limit_bytes=16 * 2**20)
TILE = jax.ShapeDtypeStruct((8, 128), F32)


def grad_of(us, cs, scale):
    u, c = jnp.concatenate(us, 0), jnp.concatenate(cs, 0)
    grad = lax.dot_general(u, c, (((0,), (0,)), ((), ())), preferred_element_type=F32)
    return (grad * scale).astype(BF16)


def gram_kernel(pairs, shifts, count, at, *refs):
    *parts, out = refs
    before = parts.pop() if len(parts) > len(shifts) else None
    rows, width = parts[0].shape
    parts = dict(zip(shifts, parts))
    full = width // 128 * 128

    def step(k, sums):
        head, tail = list(sums[0]), list(sums[1])
        here = pl.ds(pl.multiple_of(k * 16, 16), 16)
        for start in range(0, width, 128):
            x = {d: ref[here, start : min(start + 128, width)].astype(F32) for d, ref in parts.items()}
            bag = tail if start == full else head
            for n, (i, j) in enumerate(pairs):
                prod = x[i] * x[j]
                bag[n] = bag[n] + (prod[:8] + prod[8:])
        return tuple(head), tuple(tail)

    if rows % 16 == 0:
        zeros = tuple(jnp.zeros((8, 128), F32) for _ in pairs)
        short = tuple(jnp.zeros((8, width - full), F32) for _ in pairs)
        head, tail = lax.fori_loop(0, rows // 16, step, (zeros, short), unroll=2)
        sums = {p: total(h) + total(t) for p, h, t in zip(pairs, head, tail)}
    else:
        x = {d: ref[...].astype(F32) for d, ref in parts.items()}
        sums = {(i, j): total(x[i] * x[j]) for i, j in pairs}
    tile = as_tile(sums, [lax.rem(at[0] - d + count, count) for d in range(count)])
    out[...] = tile if before is None else tile + before[...]


def gram_call(parts, at, pairs, count, before=None):
    shifts = [d for d in parts if any(d in pair for pair in pairs)]
    args = [parts[d] for d in shifts] + ([] if before is None else [before])
    return pl.pallas_call(
        lambda *refs: gram_kernel(pairs, shifts, count, *refs),
        out_shape=TILE,
        in_specs=[SMEM] + [VMEM] * len(args),
        out_specs=VMEM,
        compiler_params=PARAMS,
        name="gram%d_%d" % (count, len(pairs)),
    )(at, *args)


def mix_x_kernel(shifts, at, tile, own, other, *outs):
    coefs = ordered_coefs(tile[...], [at[0], 1 - at[0]])
    rows = outs[0].shape[0]
    for shift, out in zip(shifts, outs):
        base = lax.rem(at[1] + shift, 4) * rows

        def step(k, _):
            here = pl.ds(pl.multiple_of(base + k * 32, 16), 32)
            mixed = coefs[0] * own[here].astype(F32) + coefs[1] * other[here].astype(F32)
            out[pl.ds(pl.multiple_of(k * 32, 32), 32)] = mixed.astype(BF16)
            return 0

        lax.fori_loop(0, rows // 32, step, 0)


def mix_x_call(shifts, at, tile, own, other):
    piece = jax.ShapeDtypeStruct((own.shape[0] // 4, own.shape[1]), BF16)
    return pl.pallas_call(
        lambda *refs: mix_x_kernel(shifts, *refs),
        out_shape=(piece,) * len(shifts),
        in_specs=[SMEM] + [VMEM] * 3,
        out_specs=(VMEM,) * len(shifts),
        compiler_params=PARAMS,
        name="mix_x%d" % len(shifts),
    )(at, tile, own, other)


def mix_y_kernel(at, tile, *refs):
    parts, outs, hold = refs[:4], refs[4:12], refs[12]
    coefs = ordered_coefs(tile[...], [lax.rem(at[0] - d + 4, 4) for d in range(4)])
    rows = outs[0].shape[0]
    mixed = sum(c * ref[...].astype(F32) for c, ref in zip(coefs, parts))
    for k in range(8):
        hold[k] = mixed[k * rows : (k + 1) * rows]
    for d in range(8):
        outs[d][...] = hold[lax.rem(at[1] + d, 8)].astype(BF16)


def mix_y_call(at, tile, parts):
    rows, width = parts[0].shape
    return pl.pallas_call(
        mix_y_kernel,
        out_shape=tuple(jax.ShapeDtypeStruct((rows // 8, width), BF16) for _ in range(8)),
        in_specs=[SMEM] + [VMEM] * 5,
        out_specs=(VMEM,) * 8,
        scratch_shapes=[pltpu.VMEM((8, rows // 8, width), F32)],
        compiler_params=PARAMS,
        name="mix_y",
    )(at, tile, *parts)


def mix_z_kernel(shifts, at, tile, *refs):
    parts, out = refs[:8], refs[8]
    coefs = ordered_coefs(tile[...], [lax.rem(at[0] - d + 8, 8) for d in shifts])
    out[...] = sum(c * ref[...].astype(F32) for c, ref in zip(coefs, parts)).astype(BF16)


def mix_z_call(at, tile, parts):
    return pl.pallas_call(
        lambda *refs: mix_z_kernel(list(parts), *refs),
        out_shape=jax.ShapeDtypeStruct(parts[0].shape, BF16),
        in_specs=[SMEM] + [VMEM] * 9,
        out_specs=VMEM,
        compiler_params=PARAMS,
        name="mix_z",
    )(at, tile, *parts.values())


def tied(value, *after):
    return lax.optimization_barrier((value,) + after)[0]


def on_device(context, upstream, weight):
    tokens = context.shape[0]
    half = context.shape[1] // 2
    quarter = half // 2
    z, y = lax.axis_index("z"), lax.axis_index("y")
    xl, xh, core = lax.axis_index("xl"), lax.axis_index("xh"), lax.axis_index("c")
    d_half = xl ^ xh
    pick = lambda flag, a, b: jnp.where(flag == 1, b, a)

    u0, u1 = upstream[:, :half], upstream[:, half:]
    u_own, u_rest = pick(d_half, u0, u1), pick(d_half, u1, u0)
    c0, c1 = context[:, :half], context[:, half:]
    c_own, c_rest = pick(xh, c0, c1), pick(xh, c1, c0)
    u_sib = send(u_rest, SIB)
    c_mate = send(c_rest, MATE)
    us_rest = [u_rest, send(u_rest, CHIP)]
    c_own, u_own = lax.optimization_barrier((c_own, u_own, us_rest[1]))[:2]
    c_sib = send(c_own, SIB)
    u_mate = send(u_own, MATE)
    c_opp = send(c_mate, SIB)
    u_opp = send(u_sib, MATE)

    def both_cores(value):
        return [value, send(value, CHIP)]

    def quarters(value):
        keep = pick(core, value[:, :quarter], value[:, quarter:])
        give = pick(core, value[:, quarter:], value[:, :quarter])
        return [keep, send(give, CHIP)]

    at = lambda *values: jnp.stack([v.astype(jnp.int32) for v in values])
    at_x, at_yz, at_z = at(xl, y), at(y, z), at(z)
    scale = 1.0 / (4 * tokens)
    us_own, us_mate = both_cores(u_own), both_cores(u_mate)
    other = grad_of(both_cores(u_sib) + us_mate, quarters(c_sib) + quarters(c_mate), scale)
    sums = gram_call({1: other}, at_x, [(1, 1)], 2)
    u_opp, c_opp, sums = lax.optimization_barrier((u_opp, c_opp, sums))
    own = grad_of(us_own + both_cores(u_opp), quarters(c_own) + quarters(c_opp), scale)
    sums = sum_x(gram_call({0: own, 1: other}, at_x, [(0, 0), (0, 1)], 2, sums))

    pieces = dict(zip((1, 3, 2), mix_x_call((1, 3, 2), at_x, sums, own, other)))
    parts = {d: send(pieces[d], Y_SHIFT[d]) for d in (1, 3, 2)}
    u_mate_rest = send(tied(u_rest, pieces[1]), MATE)
    parts[0] = mix_x_call((0,), at_x, tied(sums, u_mate_rest), own, other)[0]

    us_own = [tied(u, u_mate_rest) for u in us_own]
    u_a = jnp.concatenate(us_own + us_mate, 0)
    u_b = jnp.concatenate(us_rest + both_cores(u_mate_rest), 0)
    wide = jnp.concatenate([pick(d_half, u_a, u_b), pick(d_half, u_b, u_a)], 1)
    back = lax.dot_general(wide, weight, (((1,), (1,)), ((), ())), preferred_element_type=F32).astype(BF16)

    def token_rows(value):
        mine, theirs = value[:tokens], send(value[tokens:], CHIP)
        return jnp.concatenate([pick(core, mine, theirs), pick(core, theirs, mine)], 1)

    near = token_rows(back[: 2 * tokens])
    far = send(token_rows(back[2 * tokens :]), MATE)
    near, far, parts[2] = lax.optimization_barrier((near, far, parts[2]))

    parts = {d: parts[d] for d in (0, 1, 3, 2)}
    sums = gram_call(parts, at_yz, [(0, 0), (1, 1), (3, 3), (0, 1), (0, 3), (1, 3)], 4)
    sums = gram_call(parts, at_yz, [(0, 2), (1, 2), (2, 3), (2, 2)], 4, sums)
    sums = sum_x(sum_y(sums))
    pieces = mix_y_call(at_yz, sums, [parts[d] for d in range(4)])

    near_first = (0, 1, 7, 2, 6, 3, 5, 4)
    parts = {d: send(pieces[d], Z_SHIFT[d]) if d else pieces[0] for d in near_first}
    d_context = jnp.concatenate([pick(xh, near, far), pick(xh, far, near)], 1)
    d_context, parts[1] = lax.optimization_barrier((d_context, parts[1]))
    sums = gram_call(parts, at_z, [(i, j) for i in range(8) for j in range(i, 8)], 8)
    sums = sum_z(sum_x(sum_y(sums)))
    vector = mix_z_call(at_z, sums, parts)
    return d_context, send(vector, FINAL).T


def solution(mesh):
    fine = Mesh(mesh.devices.reshape(SIZES), AXES)
    return jax.shard_map(
        on_device,
        mesh=fine,
        in_specs=(P(AXES, None), P(AXES, None), P(("xh", "c"), None)),
        out_specs=(P(AXES, None), P(("xh", "c"), ("z", "y", "xl"))),
        check_vma=False,
    )
```
